32 devices in a mesh: blk: 8 (over z, x), sub: 4 (over y, core).
Axes of the slice: x: 2, y: 2, z: 4, core: 2. Of those that a mesh axis runs over, the one named last changes fastest.
Arguments:
- jacobian_tiles: bfloat16 [2048, 5, 128, 128], P(('blk', 'sub')), may hold values from -0.25 to 0.25
- column_slots: int32 [2048, 5], P(('blk', 'sub')), may hold values from 0 to 319, as said below
- bus_diagonal: float32 [2048, 128], P(('blk', 'sub')), may hold values from 1 to 4
- bus_residual: float32 [2048, 128], P(('blk', 'sub')), may hold values from -6 to 6
- gen_residual: float32 [65536], P(('blk', 'sub')), may hold values from -6 to 6
- gen_bus: int32 [65536], P(('blk', 'sub')), may hold values from 0 to 8191
- gen_emf: float32 [65536], P(('blk', 'sub')), may hold values from 0.5 to 2
- gen_angle: float32 [65536], P(('blk', 'sub')), may hold values from -3.140625 to 3.140625
- gen_inertia: float32 [65536], P(('blk', 'sub')), may hold values from 0.05 to 0.5
- gen_damping: float32 [65536], P(('blk', 'sub')), may hold values from 0.5 to 4
Outputs:
- delta_bus: float32 [2048, 128], P(('blk', 'sub'))
- delta_gen: float32 [65536], P(('blk', 'sub'))
The draws below stay inside these ranges and needn't reach their ends.
Inputs may be any that keep to these rules, and one draw needn't show every extreme that they name: `column_slots`: slot 0 of block b names b's own position in its device, b % 64; slot k >= 1 names a value in [k * 64, (k + 1) * 64).
All inputs are finite; a program needn't handle non-finite values.
Results may differ from the reference program's by a relative error of at most 0.00089.
Values may be sent and summed in bfloat16 or wider, within the bound.
A program may use at most 64 MiB of HBM per device.

```python
import math
import jax
import jax.numpy as jnp
from jax import lax

RB = 64
TILE = 128
SLOTS = 5
ITERS = 3
BLOCKS = 2048
BUSES = 262144
GEN_DEV = 2048
GENS = 65536
N_BLK = 8
N_SUB = 4


def draw_column_slots(key, part):
    within = jnp.arange(BLOCKS, dtype=jnp.int32) % RB
    picks = jax.random.randint(jax.random.fold_in(key, 17), (BLOCKS, SLOTS - 1), 0, RB, dtype=jnp.int32)
    offsets = (jnp.arange(1, SLOTS, dtype=jnp.int32) * RB)[None, :]
    return jnp.concatenate([within[:, None], picks + offsets], axis=1).astype(jnp.int32)


def set_ends(values, key, smallest, top_value):
    shape = values.shape
    index_at = [jax.random.randint(jax.random.fold_in(key, axis), (), 0, shape[axis]) for axis in range(len(shape))]
    values = values.at[tuple(index_at)].set(smallest)
    longest = shape.index(max(shape))
    index_at[longest] = (index_at[longest] + 1) % shape[longest]
    return values.at[tuple(index_at)].set(top_value)


def level_of(own_key, shape, shards, low, top_value):
    def one(axis_at, blocks):
        draws = jax.random.uniform(jax.random.fold_in(jax.random.fold_in(own_key, 6), axis_at), (blocks,), jnp.float32, low / len(shards), top_value / len(shards))
        return jnp.repeat(jnp.exp(draws), shape[axis_at] // blocks).reshape((-1,) + (1,) * (len(shape) - axis_at - 1))

    gain = one(*shards[0])
    for cut in shards[1:]:
        gain = gain * one(*cut)
    return gain


def noise(key, shape, width, bound, split=(), held_as=jnp.bfloat16):
    gain = level_of(key, shape, split, -0.22, 0.18) if split else 1.0
    values = jax.random.normal(key, shape, jnp.float32) * width * gain
    return jnp.minimum(jnp.maximum(values, -bound), bound).astype(held_as)


def setup_inputs(seed: int = 0) -> dict:
    splits = jax.random.split(jax.random.key(seed), 11)
    jacobian_tiles = noise(splits[0], (BLOCKS, SLOTS, TILE, TILE), (SLOTS * TILE) ** -0.5, 0.25, ((0, 32),))
    column_slots = draw_column_slots(jax.random.fold_in(splits[10], 71), 0)
    bus_diagonal = jnp.clip(jnp.exp(math.log(4.0) - 1.3862944 * jax.random.uniform(splits[2], (BLOCKS, TILE), jnp.float32) ** level_of(splits[2], (BLOCKS, TILE), ((0, 32),), -0.2, 0.2)), 1.0, 4.0)
    bus_residual = noise(splits[3], (BLOCKS, TILE), 1.0, 6.0, ((0, 32),), jnp.float32)
    gen_residual = noise(splits[4], (GENS,), 1.0, 6.0, ((0, 32),), jnp.float32)
    gen_bus = set_ends(jax.random.randint(splits[5], (GENS,), 0, RB * TILE), jax.random.fold_in(splits[5], 1), 0, (RB * TILE) - 1).astype(jnp.int32)
    gen_emf = jnp.clip(jnp.exp(math.log(2.0) - 1.3862944 * jax.random.uniform(splits[6], (GENS,), jnp.float32) ** level_of(splits[6], (GENS,), ((0, 32),), -0.2, 0.2)), 0.5, 2.0)
    gen_angle = jnp.clip(jax.random.uniform(splits[7], (GENS,), jnp.float32, -3.140625, 3.140625), -3.140625, 3.140625)
    gen_inertia = jnp.clip(jnp.exp(math.log(0.5) - 2.3025851 * jax.random.uniform(splits[8], (GENS,), jnp.float32) ** level_of(splits[8], (GENS,), ((0, 32),), -0.2, 0.2)), 0.05, 0.5)
    gen_damping = jnp.clip(jnp.exp(math.log(4.0) - 2.0794415 * jax.random.uniform(splits[9], (GENS,), jnp.float32) ** level_of(splits[9], (GENS,), ((0, 32),), -0.2, 0.2)), 0.5, 4.0)
    return dict(jacobian_tiles=jacobian_tiles, column_slots=column_slots, bus_diagonal=bus_diagonal, bus_residual=bus_residual, gen_residual=gen_residual, gen_bus=gen_bus, gen_emf=gen_emf, gen_angle=gen_angle, gen_inertia=gen_inertia, gen_damping=gen_damping)


def small_solve(columns, beta):
    target = [beta] + [jnp.float32(0.0) for _ in columns]
    rotations = []
    upper = []
    for index in range(len(columns)):
        column = list(columns[index])
        for prior in range(len(rotations)):
            cosine, sine = rotations[prior]
            first, second = (column[prior], column[prior + 1])
            column[prior] = cosine * first + sine * second
            column[prior + 1] = -sine * first + cosine * second
        first, second = (column[index], column[index + 1])
        radius = jnp.sqrt(first * first + second * second)
        cosine, sine = (first / radius, second / radius)
        column[index] = radius
        rotations.append((cosine, sine))
        held = target[index]
        target[index] = cosine * held
        target[index + 1] = -sine * held
        upper.append(column[:index + 1])
    count = len(columns)
    answer = [None] * count
    for index in range(count - 1, -1, -1):
        total = target[index]
        for later in range(index + 1, count):
            total = total - upper[later][index] * answer[later]
        answer[index] = total / upper[index][index]
    return answer

def reference(jacobian_tiles, column_slots, bus_diagonal, bus_residual, gen_residual, gen_bus, gen_emf, gen_angle, gen_inertia, gen_damping):
    devices = N_BLK * N_SUB
    block_ids = jnp.arange(BLOCKS, dtype=jnp.int32)
    device = block_ids // RB
    blk_index = device // N_SUB
    sub_index = device % N_SUB
    region = column_slots // RB
    local = column_slots % RB
    blk_index = blk_index[:, None]
    sub_index = sub_index[:, None]
    up_blk = (blk_index + 1) % N_BLK * N_SUB + sub_index
    down_blk = (blk_index - 1) % N_BLK * N_SUB + sub_index
    up_sub = blk_index * N_SUB + (sub_index + 1) % N_SUB
    down_sub = blk_index * N_SUB + (sub_index - 1) % N_SUB
    own = blk_index * N_SUB + sub_index
    source_dev = jnp.where(region == 0, own, jnp.where(region == 1, down_blk, jnp.where(region == 2, up_blk, jnp.where(region == 3, down_sub, up_sub))))
    source = (source_dev * RB + local).astype(jnp.int32)
    gen_ids = jnp.arange(GENS, dtype=jnp.int32)
    bus_of = (gen_ids // GEN_DEV * (RB * TILE) + gen_bus).astype(jnp.int32)
    coupling = gen_emf * jnp.cos(gen_angle)
    gen_diag = 10.0 * gen_inertia + gen_damping
    tiles_by_dev = jacobian_tiles.reshape(devices, RB, SLOTS, TILE, TILE)
    source_by_dev = source.reshape(devices, RB, SLOTS)

    def apply_op(bus_part, gen_part):
        rounded = bus_part.astype(jnp.bfloat16)

        def one_device(pair):
            tiles, picks = pair
            picked = rounded[picks].astype(jnp.float32)
            return jnp.einsum('rkij,rkj->ri', tiles.astype(jnp.float32), picked)
        product = lax.map(one_device, (tiles_by_dev, source_by_dev)).reshape(BLOCKS, TILE)
        flat = bus_part.reshape(-1)
        back = jax.ops.segment_sum(coupling * gen_part, bus_of, num_segments=BUSES)
        new_bus = bus_diagonal * bus_part + product - back.reshape(BLOCKS, TILE)
        new_gen = gen_diag * gen_part - coupling * flat[bus_of]
        return (new_bus, new_gen)

    def inner(first, second):
        return jnp.sum(first[0] * second[0]) + jnp.sum(first[1] * second[1])
    start = (-bus_residual, -gen_residual)
    beta = jnp.sqrt(inner(start, start))
    basis = [(start[0] / beta, start[1] / beta)]
    columns = []
    for index in range(ITERS):
        work = apply_op(basis[index][0], basis[index][1])
        column = []
        for prior in range(index + 1):
            weight = inner(basis[prior], work)
            work = (work[0] - weight * basis[prior][0], work[1] - weight * basis[prior][1])
            column.append(weight)
        size_now = jnp.sqrt(inner(work, work))
        column.append(size_now)
        columns.append(column)
        basis.append((work[0] / size_now, work[1] / size_now))
    answer = small_solve(columns, beta)
    delta_bus = jnp.zeros_like(bus_residual)
    delta_gen = jnp.zeros_like(gen_residual)
    for index in range(ITERS):
        delta_bus = delta_bus + answer[index] * basis[index][0]
        delta_gen = delta_gen + answer[index] * basis[index][1]
    return (delta_bus, delta_gen)
```

```python
import functools

import jax
import jax.numpy as jnp
from jax import lax
from jax.experimental import pallas as pl
from jax.experimental.pallas import tpu as pltpu
from jax.sharding import PartitionSpec as P

ITERS = 3
MESH = pl.DeviceIdType.MESH
NT = (((1,), (1,)), ((), ()))
F32 = jnp.float32
BF16 = jnp.bfloat16


def small_solve(columns, beta):
    target = [beta] + [jnp.zeros_like(beta) for _ in columns]
    rotations = []
    upper = []
    for index in range(len(columns)):
        column = list(columns[index])
        for prior in range(len(rotations)):
            cosine, sine = rotations[prior]
            first, second = (column[prior], column[prior + 1])
            column[prior] = cosine * first + sine * second
            column[prior + 1] = -sine * first + cosine * second
        first, second = (column[index], column[index + 1])
        radius = jnp.sqrt(first * first + second * second)
        cosine, sine = (first / radius, second / radius)
        column[index] = radius
        rotations.append((cosine, sine))
        held = target[index]
        target[index] = cosine * held
        target[index + 1] = -sine * held
        upper.append(column[: index + 1])
    count = len(columns)
    answer = [None] * count
    for index in range(count - 1, -1, -1):
        total = target[index]
        for later in range(index + 1, count):
            total = total - upper[later][index] * answer[later]
        answer[index] = total / upper[index][index]
    return answer


def halves(value):
    high = value.astype(BF16).astype(F32)
    return high, value - high


def fold(value):
    total = value[0:8]
    for at in range(8, value.shape[0], 8):
        total = total + value[at : at + 8]
    return total


def kernel(
    n_blk,
    n_sub,
    slots_ref,
    tiles_ref,
    diag_ref,
    bus_res_ref,
    gen_res_ref,
    gen_bus_ref,
    emf_ref,
    angle_ref,
    inertia_ref,
    damping_ref,
    out_bus_ref,
    out_gen_ref,
    own_tiles,
    far_tiles,
    sources_0,
    sources_1,
    sources_2,
    picked,
    product,
    row_hot,
    lane_hot,
    spread,
    fetched,
    sum_sub,
    sum_blk,
    own_sem,
    far_sem,
    halo_send,
    halo_recv,
    sub_send,
    sub_recv,
    blk_send,
    blk_recv,
):
    rows, tile = diag_ref.shape
    n_slots = tiles_ref.shape[1]
    groups = rows // 8
    chunks = gen_bus_ref.shape[0]
    sources = (sources_0, sources_1, sources_2)
    blk, sub = lax.axis_index("blk"), lax.axis_index("sub")

    def near(blk_step, sub_step):
        return (
            lax.rem(blk + blk_step + n_blk, n_blk),
            lax.rem(sub + sub_step + n_sub, n_sub),
        )

    def own_copy(g):
        part = pl.ds(g * 8, 8)
        return pltpu.make_async_copy(tiles_ref.at[part, 0], own_tiles.at[part], own_sem.at[g])

    def far_copy(g, k):
        part = pl.ds(g * 8, 8)
        return pltpu.make_async_copy(
            tiles_ref.at[part, k],
            far_tiles.at[part, :, pl.ds((k - 1) * tile, tile)],
            far_sem.at[g, k - 1],
        )

    for g in range(groups):
        own_copy(g).start()
    for g in range(groups):
        for k in range(1, n_slots):
            far_copy(g, k).start()

    barrier = pltpu.get_barrier_semaphore()
    for step in range(1, n_sub):
        pl.semaphore_signal(barrier, inc=1, device_id=near(0, step), device_id_type=MESH)
    for step in range(1, n_blk):
        pl.semaphore_signal(barrier, inc=1, device_id=near(step, 0), device_id_type=MESH)

    sends = []

    def send_halo(at, value):
        sources[at][0:rows, :] = value
        copies = []
        for region, device in enumerate((near(1, 0), near(-1, 0), near(0, 1), near(0, -1))):
            copy = pltpu.make_async_remote_copy(
                src_ref=sources[at].at[pl.ds(0, rows)],
                dst_ref=sources[at].at[pl.ds((region + 1) * rows, rows)],
                send_sem=halo_send.at[at, region],
                recv_sem=halo_recv.at[at, region],
                device_id=device,
                device_id_type=MESH,
            )
            copy.start()
            copies.append(copy)
        sends.extend(copies)
        return copies

    def send_sums(buffer, at, send_sem, recv_sem, count, device_at):
        copies = []
        for step in range(1, count):
            copy = pltpu.make_async_remote_copy(
                src_ref=buffer.at[at, 0],
                dst_ref=buffer.at[at, step],
                send_sem=send_sem.at[at, step],
                recv_sem=recv_sem.at[at, step],
                device_id=device_at(step),
                device_id_type=MESH,
            )
            copy.start()
            copies.append(copy)
        sends.extend(copies)
        return copies

    def start_sums(at, pairs):
        for index, (first, second) in enumerate(pairs):
            total = fold(first[0] * second[0]) + fold(first[1] * second[1])
            sum_sub[at, 0, index : index + 1, :] = jnp.sum(total, axis=0, keepdims=True)
        for index in range(len(pairs), 8):
            sum_sub[at, 0, index : index + 1, :] = jnp.zeros((1, tile), F32)
        return send_sums(sum_sub, at, sub_send, sub_recv, n_sub, lambda step: near(0, step))

    def pass_sums(at, copies):
        for copy in copies:
            copy.wait_recv()
        sum_blk[at, 0] = jnp.sum(sum_sub[at], axis=0)
        return send_sums(sum_blk, at, blk_send, blk_recv, n_blk, lambda step: near(step, 0))

    def finish_sums(at, copies, count):
        for copy in copies:
            copy.wait_recv()
        totals = jnp.sum(jnp.sum(sum_blk[at], axis=0), axis=1, keepdims=True)
        return [totals[index : index + 1, :] for index in range(count)]

    bus0 = -bus_res_ref[...]
    gen0 = -gen_res_ref[...]
    pl.semaphore_wait(barrier, n_sub + n_blk - 2)
    halo = send_halo(0, bus0)

    coupling = emf_ref[...] * jnp.cos(angle_ref[...])
    gen_diag = 10.0 * inertia_ref[...] + damping_ref[...]
    at_bus = gen_bus_ref[...]
    bus_row, bus_lane = at_bus // tile, at_bus % tile
    ids = lax.broadcasted_iota(jnp.int32, (2 * rows, tile), 0)
    upper_half = ids < rows
    row_ids = jnp.where(upper_half, ids, ids - rows)
    lane_ids = lax.broadcasted_iota(jnp.int32, (tile, tile), 0)
    for i in range(chunks):
        span = slice(i * tile, (i + 1) * tile)
        row_hot[:, span] = jnp.where(row_ids == bus_row[i : i + 1, :], 1.0, 0.0).astype(BF16)
        lane_hot[:, span] = jnp.where(lane_ids == bus_lane[i : i + 1, :], 1.0, 0.0).astype(BF16)

    pick_row = lax.broadcasted_iota(jnp.int32, (8, tile), 0)

    def diagonal_blocks(result):
        total = jnp.zeros((8, tile), F32)
        for q in range(8):
            span = slice(q * tile, (q + 1) * tile)
            total = jnp.where(pick_row == q, result[0:8, span] + result[8:16, span], total)
        return total

    def generators(vector):
        bus, gen = vector
        high, low = halves(bus)
        stacked = jnp.concatenate([high, low], axis=0).T.astype(BF16)
        weighted = coupling * gen
        w_high, w_low = halves(weighted)
        for i in range(chunks):
            span = slice(i * tile, (i + 1) * tile)
            by_lane = jnp.dot(stacked, row_hot[:, span], preferred_element_type=F32)
            fetched[i : i + 1, :] = jnp.sum(
                by_lane * lane_hot[:, span].astype(F32), axis=0, keepdims=True
            )
            both = jnp.where(upper_half, w_high[i : i + 1, :], w_low[i : i + 1, :])
            spread[:, span] = (row_hot[:, span].astype(F32) * both).astype(BF16)
        back = lax.dot_general(spread[...], lane_hot[...], NT, preferred_element_type=F32)
        new_bus = diag_ref[...] * bus - (back[0:rows] + back[rows : 2 * rows])
        new_gen = gen_diag * gen - coupling * fetched[...]
        return new_bus, new_gen

    def apply(at, vector, halo, meanwhile):
        new_bus, new_gen = generators(vector)
        product[...] = new_bus

        def own_step(g, carry):
            part = pl.ds(pl.multiple_of(g * 8, 8), 8)
            if at == 0:
                own_copy(g).wait()
            left = jnp.concatenate(halves(sources[at][part, :]), axis=0).astype(BF16)
            right = own_tiles[part].reshape(8 * tile, tile)
            result = lax.dot_general(left, right, NT, preferred_element_type=F32)
            product[part, :] += diagonal_blocks(result)
            return carry

        lax.fori_loop(0, groups, own_step, 0)
        later = meanwhile() if meanwhile else None
        for copy in halo:
            copy.wait_recv()

        def far_step(g, carry):
            part = pl.ds(pl.multiple_of(g * 8, 8), 8)
            for q in range(8):
                for k in range(1, n_slots):
                    row = sources[at][pl.ds(slots_ref[k, g * 8 + q], 1), :]
                    picked[g, q : q + 1, (k - 1) * tile : k * tile] = row
            if at == 0:
                for k in range(1, n_slots):
                    far_copy(g, k).wait()
            left = jnp.concatenate(halves(picked[g]), axis=0).astype(BF16)
            right = far_tiles[part].reshape(8 * tile, (n_slots - 1) * tile)
            result = lax.dot_general(left, right, NT, preferred_element_type=F32)
            product[part, :] += diagonal_blocks(result)
            return carry

        lax.fori_loop(0, groups, far_step, 0)
        return (product[...], new_gen), later

    def combine(terms):
        return tuple(
            functools.reduce(lambda a, b: a + b, [weight * pair[part] for weight, pair in terms])
            for part in (0, 1)
        )

    start = (bus0, gen0)
    first, _ = apply(0, start, halo, None)
    halo = send_halo(1, first[0])
    sums = start_sums(0, [(start, start), (start, first), (first, first)])
    second, later = apply(1, first, halo, lambda: pass_sums(0, sums))
    norm2, cross, size2 = finish_sums(0, later, 3)
    beta = jnp.sqrt(norm2)
    inv_beta = 1.0 / beta
    inv_norm2 = inv_beta * inv_beta
    h00 = cross * inv_norm2
    h10 = jnp.sqrt(size2 * inv_norm2 - h00 * h00)
    inv = 1.0 / h10
    v0 = combine([(inv_beta, start)])
    w0 = combine([(inv_beta, first)])
    v1 = combine([(inv, w0), (-inv * h00, v0)])
    w1 = combine([(inv * inv_beta, second), (-inv * h00, w0)])

    halo = send_halo(2, w1[0])
    sums = start_sums(1, [(v0, w1), (v1, w1), (w1, w1)])
    third, later = apply(2, w1, halo, lambda: pass_sums(1, sums))
    h01, h11, size2 = finish_sums(1, later, 3)
    h21 = jnp.sqrt(size2 - h01 * h01 - h11 * h11)
    inv = 1.0 / h21
    v2 = combine([(inv, w1), (-inv * h01, v0), (-inv * h11, v1)])
    w2 = combine([(inv, third), (-inv * h01, w0), (-inv * h11, w1)])

    sums = start_sums(2, [(v0, w2), (v1, w2), (v2, w2), (w2, w2)])
    later = pass_sums(2, sums)
    h02, h12, h22, size2 = finish_sums(2, later, 4)
    h32 = jnp.sqrt(size2 - h02 * h02 - h12 * h12 - h22 * h22)

    answer = small_solve([[h00, h10], [h01, h11, h21], [h02, h12, h22, h32]], beta)
    out_bus_ref[...], out_gen_ref[...] = combine(list(zip(answer, (v0, v1, v2))))
    for copy in sends:
        copy.wait_send()


def on_device(
    n_blk,
    n_sub,
    jacobian_tiles,
    column_slots,
    bus_diagonal,
    bus_residual,
    gen_residual,
    gen_bus,
    gen_emf,
    gen_angle,
    gen_inertia,
    gen_damping,
):
    rows, n_slots, tile, _ = jacobian_tiles.shape
    gens = gen_bus.shape[0]
    chunks = gens // tile
    groups = rows // 8
    far = n_slots - 1
    generator = [
        part.reshape(chunks, tile)
        for part in (gen_residual, gen_bus, gen_emf, gen_angle, gen_inertia, gen_damping)
    ]
    vmem = pl.BlockSpec(memory_space=pltpu.VMEM)
    dma = pltpu.SemaphoreType.DMA
    delta_bus, delta_gen = pl.pallas_call(
        functools.partial(kernel, n_blk, n_sub),
        out_shape=(
            jax.ShapeDtypeStruct((rows, tile), F32),
            jax.ShapeDtypeStruct((chunks, tile), F32),
        ),
        in_specs=[pl.BlockSpec(memory_space=pltpu.SMEM), pl.BlockSpec(memory_space=pl.ANY)]
        + [vmem] * 8,
        out_specs=(vmem, vmem),
        scratch_shapes=[
            pltpu.VMEM((rows, tile, tile), BF16),
            pltpu.VMEM((rows, tile, far * tile), BF16),
            *[pltpu.VMEM((n_slots * rows, tile), F32)] * ITERS,
            pltpu.VMEM((groups, 8, far * tile), F32),
            pltpu.VMEM((rows, tile), F32),
            pltpu.VMEM((2 * rows, gens), BF16),
            pltpu.VMEM((tile, gens), BF16),
            pltpu.VMEM((2 * rows, gens), BF16),
            pltpu.VMEM((chunks, tile), F32),
            pltpu.VMEM((ITERS, n_sub, 8, tile), F32),
            pltpu.VMEM((ITERS, n_blk, 8, tile), F32),
            dma((groups,)),
            dma((groups, far)),
            dma((ITERS, 4)),
            dma((ITERS, 4)),
            dma((ITERS, n_sub)),
            dma((ITERS, n_sub)),
            dma((ITERS, n_blk)),
            dma((ITERS, n_blk)),
        ],
        compiler_params=pltpu.CompilerParams(
            collective_id=0, has_side_effects=True, vmem_limit_bytes=48 * 1024 * 1024
        ),
    )(column_slots.T, jacobian_tiles, bus_diagonal, bus_residual, *generator)
    return delta_bus, delta_gen.reshape(gens)


def solution(mesh):
    both = ("blk", "sub")
    in_specs = (
        P(both, None, None, None),
        P(both, None),
        P(both, None),
        P(both, None),
        P(both),
        P(both),
        P(both),
        P(both),
        P(both),
        P(both),
    )
    return jax.shard_map(
        functools.partial(on_device, mesh.shape["blk"], mesh.shape["sub"]),
        mesh=mesh,
        in_specs=in_specs,
        out_specs=(P(both, None), P(both)),
        check_vma=False,
    )
```

```python
import functools

import jax
import jax.numpy as jnp
from jax import lax
from jax.experimental import pallas as pl
from jax.experimental.pallas import tpu as pltpu
from jax.sharding import PartitionSpec as P

ITERS = 3
MESH = pl.DeviceIdType.MESH
NT = (((1,), (1,)), ((), ()))
F32 = jnp.float32
BF16 = jnp.bfloat16


def small_solve(columns, beta):
    target = [beta] + [jnp.zeros_like(beta) for _ in columns]
    rotations = []
    upper = []
    for index in range(len(columns)):
        column = list(columns[index])
        for prior in range(len(rotations)):
            cosine, sine = rotations[prior]
            first, second = (column[prior], column[prior + 1])
            column[prior] = cosine * first + sine * second
            column[prior + 1] = -sine * first + cosine * second
        first, second = (column[index], column[index + 1])
        radius = jnp.sqrt(first * first + second * second)
        cosine, sine = (first / radius, second / radius)
        column[index] = radius
        rotations.append((cosine, sine))
        held = target[index]
        target[index] = cosine * held
        target[index + 1] = -sine * held
        upper.append(column[: index + 1])
    count = len(columns)
    answer = [None] * count
    for index in range(count - 1, -1, -1):
        total = target[index]
        for later in range(index + 1, count):
            total = total - upper[later][index] * answer[later]
        answer[index] = total / upper[index][index]
    return answer


def halves(value):
    high = value.astype(BF16).astype(F32)
    return high, value - high


def fold(value):
    total = value[0:8]
    for at in range(8, value.shape[0], 8):
        total = total + value[at : at + 8]
    return total


def kernel(n_blk, n_sub, tiles_ref, *refs):
    in_hbm, refs = refs[:9], refs[9:]
    out_bus_ref, out_gen_ref = refs[:2]
    in_place, small_sem = refs[2:11], refs[11]
    (
        own_tiles,
        far_tiles,
        sources_0,
        sources_1,
        sources_2,
        picked,
        product,
        row_hot,
        lane_hot,
        spread,
        fetched,
        sum_sub,
        sum_blk,
        own_sem,
        far_sem,
        halo_send,
        halo_recv,
        sub_send,
        sub_recv,
        blk_send,
        blk_recv,
    ) = refs[12:]
    (
        bus_res_ref,
        gen_res_ref,
        gen_bus_ref,
        emf_ref,
        angle_ref,
        inertia_ref,
        damping_ref,
        diag_ref,
        slots_ref,
    ) = in_place
    small = [
        pltpu.make_async_copy(here, there, small_sem.at[index])
        for index, (here, there) in enumerate(zip(in_hbm, in_place))
    ]
    for copy in small:
        copy.start()
    rows, tile = diag_ref.shape
    n_slots = tiles_ref.shape[1]
    groups = rows // 8
    chunks = gen_bus_ref.shape[0]
    sources = (sources_0, sources_1, sources_2)
    blk, sub = lax.axis_index("blk"), lax.axis_index("sub")

    def near(blk_step, sub_step):
        return (
            lax.rem(blk + blk_step + n_blk, n_blk),
            lax.rem(sub + sub_step + n_sub, n_sub),
        )

    def own_copy(g):
        part = pl.ds(g * 8, 8)
        return pltpu.make_async_copy(tiles_ref.at[part, 0], own_tiles.at[part], own_sem.at[g])

    def far_copy(g, k):
        part = pl.ds(g * 8, 8)
        return pltpu.make_async_copy(
            tiles_ref.at[part, k],
            far_tiles.at[part, :, pl.ds((k - 1) * tile, tile)],
            far_sem.at[g, k - 1],
        )

    for g in range(groups):
        own_copy(g).start()
    for g in range(groups):
        for k in range(1, n_slots):
            far_copy(g, k).start()

    barrier = pltpu.get_barrier_semaphore()
    for step in range(1, n_sub):
        pl.semaphore_signal(barrier, inc=1, device_id=near(0, step), device_id_type=MESH)
    for step in range(1, n_blk):
        pl.semaphore_signal(barrier, inc=1, device_id=near(step, 0), device_id_type=MESH)

    sends = []

    def send_halo(at, value):
        sources[at][0:rows, :] = value
        copies = []
        for region, device in enumerate((near(1, 0), near(-1, 0), near(0, 1), near(0, -1))):
            copy = pltpu.make_async_remote_copy(
                src_ref=sources[at].at[pl.ds(0, rows)],
                dst_ref=sources[at].at[pl.ds((region + 1) * rows, rows)],
                send_sem=halo_send.at[at, region],
                recv_sem=halo_recv.at[at, region],
                device_id=device,
                device_id_type=MESH,
            )
            copy.start()
            copies.append(copy)
        sends.extend(copies)
        return copies

    def send_sums(buffer, at, send_sem, recv_sem, count, device_at):
        copies = []
        for step in range(1, count):
            copy = pltpu.make_async_remote_copy(
                src_ref=buffer.at[at, 0],
                dst_ref=buffer.at[at, step],
                send_sem=send_sem.at[at, step],
                recv_sem=recv_sem.at[at, step],
                device_id=device_at(step),
                device_id_type=MESH,
            )
            copy.start()
            copies.append(copy)
        sends.extend(copies)
        return copies

    def start_sums(at, pairs):
        for index, (first, second) in enumerate(pairs):
            total = fold(first[0] * second[0]) + fold(first[1] * second[1])
            sum_sub[at, 0, index : index + 1, :] = jnp.sum(total, axis=0, keepdims=True)
        for index in range(len(pairs), 8):
            sum_sub[at, 0, index : index + 1, :] = jnp.zeros((1, tile), F32)
        return send_sums(sum_sub, at, sub_send, sub_recv, n_sub, lambda step: near(0, step))

    def pass_sums(at, copies):
        for copy in copies:
            copy.wait_recv()
        sum_blk[at, 0] = jnp.sum(sum_sub[at], axis=0)
        return send_sums(sum_blk, at, blk_send, blk_recv, n_blk, lambda step: near(step, 0))

    def finish_sums(at, copies, count):
        for copy in copies:
            copy.wait_recv()
        totals = jnp.sum(jnp.sum(sum_blk[at], axis=0), axis=1, keepdims=True)
        return [totals[index : index + 1, :] for index in range(count)]

    for copy in small:
        copy.wait()
    bus0 = -bus_res_ref[...]
    gen0 = -gen_res_ref[...]
    pl.semaphore_wait(barrier, n_sub + n_blk - 2)
    halo = send_halo(0, bus0)

    coupling = emf_ref[...] * jnp.cos(angle_ref[...])
    gen_diag = 10.0 * inertia_ref[...] + damping_ref[...]
    at_bus = gen_bus_ref[...]
    bus_row, bus_lane = at_bus // tile, at_bus % tile
    ids = lax.broadcasted_iota(jnp.int32, (2 * rows, tile), 0)
    upper_half = ids < rows
    row_ids = jnp.where(upper_half, ids, ids - rows)
    lane_ids = lax.broadcasted_iota(jnp.int32, (tile, tile), 0)
    for i in range(chunks):
        span = slice(i * tile, (i + 1) * tile)
        row_hot[:, span] = jnp.where(row_ids == bus_row[i : i + 1, :], 1.0, 0.0).astype(BF16)
        lane_hot[:, span] = jnp.where(lane_ids == bus_lane[i : i + 1, :], 1.0, 0.0).astype(BF16)

    pick_row = lax.broadcasted_iota(jnp.int32, (8, tile), 0)

    def diagonal_blocks(result):
        total = jnp.zeros((8, tile), F32)
        for q in range(8):
            span = slice(q * tile, (q + 1) * tile)
            total = jnp.where(pick_row == q, result[0:8, span] + result[8:16, span], total)
        return total

    def generators(vector):
        bus, gen = vector
        high, low = halves(bus)
        stacked = jnp.concatenate([high, low], axis=0).T.astype(BF16)
        weighted = coupling * gen
        w_high, w_low = halves(weighted)
        for i in range(chunks):
            span = slice(i * tile, (i + 1) * tile)
            by_lane = jnp.dot(stacked, row_hot[:, span], preferred_element_type=F32)
            fetched[i : i + 1, :] = jnp.sum(
                by_lane * lane_hot[:, span].astype(F32), axis=0, keepdims=True
            )
            both = jnp.where(upper_half, w_high[i : i + 1, :], w_low[i : i + 1, :])
            spread[:, span] = (row_hot[:, span].astype(F32) * both).astype(BF16)
        back = lax.dot_general(spread[...], lane_hot[...], NT, preferred_element_type=F32)
        new_bus = diag_ref[...] * bus - (back[0:rows] + back[rows : 2 * rows])
        new_gen = gen_diag * gen - coupling * fetched[...]
        return new_bus, new_gen

    def apply(at, vector, halo, meanwhile):
        new_bus, new_gen = generators(vector)
        product[...] = new_bus

        def own_step(g, carry):
            part = pl.ds(pl.multiple_of(g * 8, 8), 8)
            if at == 0:
                own_copy(g).wait()
            left = jnp.concatenate(halves(sources[at][part, :]), axis=0).astype(BF16)
            right = own_tiles[part].reshape(8 * tile, tile)
            result = lax.dot_general(left, right, NT, preferred_element_type=F32)
            product[part, :] += diagonal_blocks(result)
            return carry

        lax.fori_loop(0, groups, own_step, 0)
        later = meanwhile() if meanwhile else None
        for copy in halo:
            copy.wait_recv()

        def far_step(g, carry):
            part = pl.ds(pl.multiple_of(g * 8, 8), 8)
            for q in range(8):
                for k in range(1, n_slots):
                    row = sources[at][pl.ds(slots_ref[k, g * 8 + q], 1), :]
                    picked[g, q : q + 1, (k - 1) * tile : k * tile] = row
            if at == 0:
                for k in range(1, n_slots):
                    far_copy(g, k).wait()
            left = jnp.concatenate(halves(picked[g]), axis=0).astype(BF16)
            right = far_tiles[part].reshape(8 * tile, (n_slots - 1) * tile)
            result = lax.dot_general(left, right, NT, preferred_element_type=F32)
            product[part, :] += diagonal_blocks(result)
            return carry

        lax.fori_loop(0, groups, far_step, 0)
        return (product[...], new_gen), later

    def combine(terms):
        return tuple(
            functools.reduce(lambda a, b: a + b, [weight * pair[part] for weight, pair in terms])
            for part in (0, 1)
        )

    start = (bus0, gen0)
    first, _ = apply(0, start, halo, None)
    halo = send_halo(1, first[0])
    sums = start_sums(0, [(start, start), (start, first), (first, first)])
    second, later = apply(1, first, halo, lambda: pass_sums(0, sums))
    norm2, cross, size2 = finish_sums(0, later, 3)
    beta = jnp.sqrt(norm2)
    inv_beta = 1.0 / beta
    inv_norm2 = inv_beta * inv_beta
    h00 = cross * inv_norm2
    h10 = jnp.sqrt(size2 * inv_norm2 - h00 * h00)
    inv = 1.0 / h10
    v0 = combine([(inv_beta, start)])
    w0 = combine([(inv_beta, first)])
    v1 = combine([(inv, w0), (-inv * h00, v0)])
    w1 = combine([(inv * inv_beta, second), (-inv * h00, w0)])

    halo = send_halo(2, w1[0])
    sums = start_sums(1, [(v0, w1), (v1, w1), (w1, w1)])
    third, later = apply(2, w1, halo, lambda: pass_sums(1, sums))
    h01, h11, size2 = finish_sums(1, later, 3)
    h21 = jnp.sqrt(size2 - h01 * h01 - h11 * h11)
    inv = 1.0 / h21
    v2 = combine([(inv, w1), (-inv * h01, v0), (-inv * h11, v1)])
    w2 = combine([(inv, third), (-inv * h01, w0), (-inv * h11, w1)])

    sums = start_sums(2, [(v0, w2), (v1, w2), (v2, w2), (w2, w2)])
    later = pass_sums(2, sums)
    h02, h12, h22, size2 = finish_sums(2, later, 4)
    h32 = jnp.sqrt(size2 - h02 * h02 - h12 * h12 - h22 * h22)

    answer = small_solve([[h00, h10], [h01, h11, h21], [h02, h12, h22, h32]], beta)
    out_bus_ref[...], out_gen_ref[...] = combine(list(zip(answer, (v0, v1, v2))))
    for copy in sends:
        copy.wait_send()


def on_device(
    n_blk,
    n_sub,
    jacobian_tiles,
    column_slots,
    bus_diagonal,
    bus_residual,
    gen_residual,
    gen_bus,
    gen_emf,
    gen_angle,
    gen_inertia,
    gen_damping,
):
    rows, n_slots, tile, _ = jacobian_tiles.shape
    gens = gen_bus.shape[0]
    chunks = gens // tile
    groups = rows // 8
    far = n_slots - 1
    generator = [
        part.reshape(chunks, tile)
        for part in (gen_residual, gen_bus, gen_emf, gen_angle, gen_inertia, gen_damping)
    ]
    vmem = pl.BlockSpec(memory_space=pltpu.VMEM)
    dma = pltpu.SemaphoreType.DMA
    delta_bus, delta_gen = pl.pallas_call(
        functools.partial(kernel, n_blk, n_sub),
        out_shape=(
            jax.ShapeDtypeStruct((rows, tile), F32),
            jax.ShapeDtypeStruct((chunks, tile), F32),
        ),
        in_specs=[pl.BlockSpec(memory_space=pltpu.HBM)] * 10,
        out_specs=(vmem, vmem),
        scratch_shapes=[
            pltpu.VMEM((rows, tile), F32),
            pltpu.VMEM((chunks, tile), F32),
            pltpu.VMEM((chunks, tile), jnp.int32),
            *[pltpu.VMEM((chunks, tile), F32)] * 4,
            pltpu.VMEM((rows, tile), F32),
            pltpu.SMEM((n_slots, rows), jnp.int32),
            dma((9,)),
            pltpu.VMEM((rows, tile, tile), BF16),
            pltpu.VMEM((rows, tile, far * tile), BF16),
            *[pltpu.VMEM((n_slots * rows, tile), F32)] * ITERS,
            pltpu.VMEM((groups, 8, far * tile), F32),
            pltpu.VMEM((rows, tile), F32),
            pltpu.VMEM((2 * rows, gens), BF16),
            pltpu.VMEM((tile, gens), BF16),
            pltpu.VMEM((2 * rows, gens), BF16),
            pltpu.VMEM((chunks, tile), F32),
            pltpu.VMEM((ITERS, n_sub, 8, tile), F32),
            pltpu.VMEM((ITERS, n_blk, 8, tile), F32),
            dma((groups,)),
            dma((groups, far)),
            dma((ITERS, 4)),
            dma((ITERS, 4)),
            dma((ITERS, n_sub)),
            dma((ITERS, n_sub)),
            dma((ITERS, n_blk)),
            dma((ITERS, n_blk)),
        ],
        compiler_params=pltpu.CompilerParams(
            collective_id=0, has_side_effects=True, vmem_limit_bytes=60 * 1024 * 1024
        ),
    )(jacobian_tiles, bus_residual, *generator, bus_diagonal, column_slots.T)
    return delta_bus, delta_gen.reshape(gens)


def solution(mesh):
    both = ("blk", "sub")
    in_specs = (
        P(both, None, None, None),
        P(both, None),
        P(both, None),
        P(both, None),
        P(both),
        P(both),
        P(both),
        P(both),
        P(both),
        P(both),
    )
    return jax.shard_map(
        functools.partial(on_device, mesh.shape["blk"], mesh.shape["sub"]),
        mesh=mesh,
        in_specs=in_specs,
        out_specs=(P(both, None), P(both)),
        check_vma=False,
    )
```

```python
import functools

import jax
import jax.numpy as jnp
from jax import lax
from jax.experimental import pallas as pl
from jax.experimental.pallas import tpu as pltpu
from jax.sharding import PartitionSpec as P

ITERS = 3
MESH = pl.DeviceIdType.MESH
NT = (((1,), (1,)), ((), ()))
F32 = jnp.float32
BF16 = jnp.bfloat16


def small_solve(columns, beta):
    target = [beta] + [jnp.zeros_like(beta) for _ in columns]
    rotations = []
    upper = []
    for index in range(len(columns)):
        column = list(columns[index])
        for prior in range(len(rotations)):
            cosine, sine = rotations[prior]
            first, second = (column[prior], column[prior + 1])
            column[prior] = cosine * first + sine * second
            column[prior + 1] = -sine * first + cosine * second
        first, second = (column[index], column[index + 1])
        radius = jnp.sqrt(first * first + second * second)
        cosine, sine = (first / radius, second / radius)
        column[index] = radius
        rotations.append((cosine, sine))
        held = target[index]
        target[index] = cosine * held
        target[index + 1] = -sine * held
        upper.append(column[: index + 1])
    count = len(columns)
    answer = [None] * count
    for index in range(count - 1, -1, -1):
        total = target[index]
        for later in range(index + 1, count):
            total = total - upper[later][index] * answer[later]
        answer[index] = total / upper[index][index]
    return answer


def halves(value):
    high = value.astype(BF16).astype(F32)
    return high, value - high


def fold(value):
    total = value[0:8]
    for at in range(8, value.shape[0], 8):
        total = total + value[at : at + 8]
    return total


def kernel(n_blk, n_sub, tiles_ref, *refs):
    in_hbm, refs = refs[:9], refs[9:]
    out_bus_ref, out_gen_ref = refs[:2]
    in_place, small_sem = refs[2:11], refs[11]
    (
        own_tiles,
        far_tiles,
        sources_0,
        sources_1,
        sources_2,
        picked,
        product,
        row_hot,
        lane_hot,
        spread,
        fetched,
        sum_sub,
        sum_blk,
        own_sem,
        far_sem,
        halo_send,
        halo_recv,
        sub_send,
        sub_recv,
        blk_send,
        blk_recv,
    ) = refs[12:]
    (
        bus_res_ref,
        gen_res_ref,
        gen_bus_ref,
        emf_ref,
        angle_ref,
        inertia_ref,
        damping_ref,
        diag_ref,
        slots_ref,
    ) = in_place
    small = [
        pltpu.make_async_copy(here, there, small_sem.at[index])
        for index, (here, there) in enumerate(zip(in_hbm, in_place))
    ]
    for copy in small:
        copy.start()
    rows, tile = diag_ref.shape
    n_slots = tiles_ref.shape[1]
    groups = rows // 8
    half = groups // 2
    chunks = gen_bus_ref.shape[0]
    sources = (sources_0, sources_1, sources_2)
    blk, sub = lax.axis_index("blk"), lax.axis_index("sub")

    def near(blk_step, sub_step):
        return (
            lax.rem(blk + blk_step + n_blk, n_blk),
            lax.rem(sub + sub_step + n_sub, n_sub),
        )

    def own_copy(g):
        part = pl.ds(g * 8, 8)
        there = own_tiles.at[
            pl.ds(g % half * 8, 8), :, pl.ds(pl.multiple_of(g // half * tile, tile), tile)
        ]
        return pltpu.make_async_copy(tiles_ref.at[part, 0], there, own_sem.at[g])

    def far_copy(g, k):
        part = pl.ds(g * 8, 8)
        return pltpu.make_async_copy(
            tiles_ref.at[part, k],
            far_tiles.at[part, :, pl.ds((k - 1) * tile, tile)],
            far_sem.at[g, k - 1],
        )

    for g in range(groups):
        own_copy(g).start()
    for g in range(groups):
        for k in range(1, n_slots):
            far_copy(g, k).start()

    barrier = pltpu.get_barrier_semaphore()
    for step in range(1, n_sub):
        pl.semaphore_signal(barrier, inc=1, device_id=near(0, step), device_id_type=MESH)
    for step in range(1, n_blk):
        pl.semaphore_signal(barrier, inc=1, device_id=near(step, 0), device_id_type=MESH)

    sends = []

    def send_halo(at, value):
        sources[at][0:rows, :] = value
        copies = []
        for region, device in enumerate((near(1, 0), near(-1, 0), near(0, 1), near(0, -1))):
            copy = pltpu.make_async_remote_copy(
                src_ref=sources[at].at[pl.ds(0, rows)],
                dst_ref=sources[at].at[pl.ds((region + 1) * rows, rows)],
                send_sem=halo_send.at[at, region],
                recv_sem=halo_recv.at[at, region],
                device_id=device,
                device_id_type=MESH,
            )
            copy.start()
            copies.append(copy)
        sends.extend(copies)
        return copies

    def send_sums(buffer, at, send_sem, recv_sem, count, device_at):
        copies = []
        for step in range(1, count):
            copy = pltpu.make_async_remote_copy(
                src_ref=buffer.at[at, 0],
                dst_ref=buffer.at[at, step],
                send_sem=send_sem.at[at, step],
                recv_sem=recv_sem.at[at, step],
                device_id=device_at(step),
                device_id_type=MESH,
            )
            copy.start()
            copies.append(copy)
        sends.extend(copies)
        return copies

    def start_sums(at, pairs):
        for index, (first, second) in enumerate(pairs):
            total = fold(first[0] * second[0]) + fold(first[1] * second[1])
            sum_sub[at, 0, index : index + 1, :] = jnp.sum(total, axis=0, keepdims=True)
        for index in range(len(pairs), 8):
            sum_sub[at, 0, index : index + 1, :] = jnp.zeros((1, tile), F32)
        return send_sums(sum_sub, at, sub_send, sub_recv, n_sub, lambda step: near(0, step))

    def pass_sums(at, copies):
        for copy in copies:
            copy.wait_recv()
        sum_blk[at, 0] = jnp.sum(sum_sub[at], axis=0)
        return send_sums(sum_blk, at, blk_send, blk_recv, n_blk, lambda step: near(step, 0))

    def finish_sums(at, copies, count):
        for copy in copies:
            copy.wait_recv()
        totals = jnp.sum(jnp.sum(sum_blk[at], axis=0), axis=1, keepdims=True)
        return [totals[index : index + 1, :] for index in range(count)]

    for copy in small:
        copy.wait()
    bus0 = -bus_res_ref[...]
    gen0 = -gen_res_ref[...]
    pl.semaphore_wait(barrier, n_sub + n_blk - 2)
    halo = send_halo(0, bus0)

    coupling = emf_ref[...] * jnp.cos(angle_ref[...])
    gen_diag = 10.0 * inertia_ref[...] + damping_ref[...]
    at_bus = gen_bus_ref[...]
    bus_row, bus_lane = at_bus // tile, at_bus % tile
    ids = lax.broadcasted_iota(jnp.int32, (2 * rows, tile), 0)
    upper_half = ids < rows
    row_ids = jnp.where(upper_half, ids, ids - rows)
    lane_ids = lax.broadcasted_iota(jnp.int32, (tile, tile), 0)
    for i in range(chunks):
        span = slice(i * tile, (i + 1) * tile)
        row_hot[:, span] = jnp.where(row_ids == bus_row[i : i + 1, :], 1.0, 0.0).astype(BF16)
        lane_hot[:, span] = jnp.where(lane_ids == bus_lane[i : i + 1, :], 1.0, 0.0).astype(BF16)

    pick_row = lax.broadcasted_iota(jnp.int32, (8, tile), 0)

    def diagonal_blocks(result):
        total = jnp.zeros((8, tile), F32)
        for q in range(8):
            span = slice(q * tile, (q + 1) * tile)
            total = jnp.where(pick_row == q, result[0:8, span] + result[8:16, span], total)
        return total

    def generators(vector):
        bus, gen = vector
        high, low = halves(bus)
        stacked = jnp.concatenate([high, low], axis=0).T.astype(BF16)
        weighted = coupling * gen
        w_high, w_low = halves(weighted)
        for i in range(chunks):
            span = slice(i * tile, (i + 1) * tile)
            by_lane = jnp.dot(stacked, row_hot[:, span], preferred_element_type=F32)
            fetched[i : i + 1, :] = jnp.sum(
                by_lane * lane_hot[:, span].astype(F32), axis=0, keepdims=True
            )
            both = jnp.where(upper_half, w_high[i : i + 1, :], w_low[i : i + 1, :])
            spread[:, span] = (row_hot[:, span].astype(F32) * both).astype(BF16)
        back = lax.dot_general(spread[...], lane_hot[...], NT, preferred_element_type=F32)
        new_bus = diag_ref[...] * bus - (back[0:rows] + back[rows : 2 * rows])
        new_gen = gen_diag * gen - coupling * fetched[...]
        return new_bus, new_gen

    def apply(at, vector, halo, meanwhile):
        new_bus, new_gen = generators(vector)
        product[...] = new_bus

        def own_step(g, carry):
            part = pl.ds(pl.multiple_of(g * 8, 8), 8)
            other = pl.ds(pl.multiple_of((g + half) * 8, 8), 8)
            if at == 0:
                own_copy(g).wait()
                own_copy(g + half).wait()
            first = jnp.concatenate(halves(sources[at][part, :]), axis=0)
            second = jnp.concatenate(halves(sources[at][other, :]), axis=0)
            none = jnp.zeros_like(first)
            left = jnp.concatenate(
                [
                    jnp.concatenate([first, none], axis=1),
                    jnp.concatenate([none, second], axis=1),
                ],
                axis=0,
            ).astype(BF16)
            right = own_tiles[part].reshape(8 * tile, 2 * tile)
            result = lax.dot_general(left, right, NT, preferred_element_type=F32)
            product[part, :] += diagonal_blocks(result[0:16])
            product[other, :] += diagonal_blocks(result[16:32])
            return carry

        lax.fori_loop(0, half, own_step, 0)
        later = meanwhile() if meanwhile else None
        for copy in halo:
            copy.wait_recv()

        def far_step(g, carry):
            part = pl.ds(pl.multiple_of(g * 8, 8), 8)
            for q in range(8):
                for k in range(1, n_slots):
                    row = sources[at][pl.ds(slots_ref[k, g * 8 + q], 1), :]
                    picked[g, q : q + 1, (k - 1) * tile : k * tile] = row
            if at == 0:
                for k in range(1, n_slots):
                    far_copy(g, k).wait()
            left = jnp.concatenate(halves(picked[g]), axis=0).astype(BF16)
            right = far_tiles[part].reshape(8 * tile, (n_slots - 1) * tile)
            result = lax.dot_general(left, right, NT, preferred_element_type=F32)
            product[part, :] += diagonal_blocks(result)
            return carry

        lax.fori_loop(0, groups, far_step, 0)
        return (product[...], new_gen), later

    def combine(terms):
        return tuple(
            functools.reduce(lambda a, b: a + b, [weight * pair[part] for weight, pair in terms])
            for part in (0, 1)
        )

    start = (bus0, gen0)
    first, _ = apply(0, start, halo, None)
    halo = send_halo(1, first[0])
    sums = start_sums(0, [(start, start), (start, first), (first, first)])
    second, later = apply(1, first, halo, lambda: pass_sums(0, sums))
    norm2, cross, size2 = finish_sums(0, later, 3)
    beta = jnp.sqrt(norm2)
    inv_beta = 1.0 / beta
    inv_norm2 = inv_beta * inv_beta
    h00 = cross * inv_norm2
    h10 = jnp.sqrt(size2 * inv_norm2 - h00 * h00)
    inv = 1.0 / h10
    v0 = combine([(inv_beta, start)])
    w0 = combine([(inv_beta, first)])
    v1 = combine([(inv, w0), (-inv * h00, v0)])
    w1 = combine([(inv * inv_beta, second), (-inv * h00, w0)])

    halo = send_halo(2, w1[0])
    sums = start_sums(1, [(v0, w1), (v1, w1), (w1, w1)])
    third, later = apply(2, w1, halo, lambda: pass_sums(1, sums))
    h01, h11, size2 = finish_sums(1, later, 3)
    h21 = jnp.sqrt(size2 - h01 * h01 - h11 * h11)
    inv = 1.0 / h21
    v2 = combine([(inv, w1), (-inv * h01, v0), (-inv * h11, v1)])
    w2 = combine([(inv, third), (-inv * h01, w0), (-inv * h11, w1)])

    sums = start_sums(2, [(v0, w2), (v1, w2), (v2, w2), (w2, w2)])
    later = pass_sums(2, sums)
    h02, h12, h22, size2 = finish_sums(2, later, 4)
    h32 = jnp.sqrt(size2 - h02 * h02 - h12 * h12 - h22 * h22)

    answer = small_solve([[h00, h10], [h01, h11, h21], [h02, h12, h22, h32]], beta)
    out_bus_ref[...], out_gen_ref[...] = combine(list(zip(answer, (v0, v1, v2))))
    for copy in sends:
        copy.wait_send()


def on_device(
    n_blk,
    n_sub,
    jacobian_tiles,
    column_slots,
    bus_diagonal,
    bus_residual,
    gen_residual,
    gen_bus,
    gen_emf,
    gen_angle,
    gen_inertia,
    gen_damping,
):
    rows, n_slots, tile, _ = jacobian_tiles.shape
    gens = gen_bus.shape[0]
    chunks = gens // tile
    groups = rows // 8
    far = n_slots - 1
    generator = [
        part.reshape(chunks, tile)
        for part in (gen_residual, gen_bus, gen_emf, gen_angle, gen_inertia, gen_damping)
    ]
    vmem = pl.BlockSpec(memory_space=pltpu.VMEM)
    dma = pltpu.SemaphoreType.DMA
    delta_bus, delta_gen = pl.pallas_call(
        functools.partial(kernel, n_blk, n_sub),
        out_shape=(
            jax.ShapeDtypeStruct((rows, tile), F32),
            jax.ShapeDtypeStruct((chunks, tile), F32),
        ),
        in_specs=[pl.BlockSpec(memory_space=pltpu.HBM)] * 10,
        out_specs=(vmem, vmem),
        scratch_shapes=[
            pltpu.VMEM((rows, tile), F32),
            pltpu.VMEM((chunks, tile), F32),
            pltpu.VMEM((chunks, tile), jnp.int32),
            *[pltpu.VMEM((chunks, tile), F32)] * 4,
            pltpu.VMEM((rows, tile), F32),
            pltpu.SMEM((n_slots, rows), jnp.int32),
            dma((9,)),
            pltpu.VMEM((rows // 2, tile, 2 * tile), BF16),
            pltpu.VMEM((rows, tile, far * tile), BF16),
            *[pltpu.VMEM((n_slots * rows, tile), F32)] * ITERS,
            pltpu.VMEM((groups, 8, far * tile), F32),
            pltpu.VMEM((rows, tile), F32),
            pltpu.VMEM((2 * rows, gens), BF16),
            pltpu.VMEM((tile, gens), BF16),
            pltpu.VMEM((2 * rows, gens), BF16),
            pltpu.VMEM((chunks, tile), F32),
            pltpu.VMEM((ITERS, n_sub, 8, tile), F32),
            pltpu.VMEM((ITERS, n_blk, 8, tile), F32),
            dma((groups,)),
            dma((groups, far)),
            dma((ITERS, 4)),
            dma((ITERS, 4)),
            dma((ITERS, n_sub)),
            dma((ITERS, n_sub)),
            dma((ITERS, n_blk)),
            dma((ITERS, n_blk)),
        ],
        compiler_params=pltpu.CompilerParams(
            collective_id=0, has_side_effects=True, vmem_limit_bytes=60 * 1024 * 1024
        ),
    )(jacobian_tiles, bus_residual, *generator, bus_diagonal, column_slots.T)
    return delta_bus, delta_gen.reshape(gens)


def solution(mesh):
    both = ("blk", "sub")
    in_specs = (
        P(both, None, None, None),
        P(both, None),
        P(both, None),
        P(both, None),
        P(both),
        P(both),
        P(both),
        P(both),
        P(both),
        P(both),
    )
    return jax.shard_map(
        functools.partial(on_device, mesh.shape["blk"], mesh.shape["sub"]),
        mesh=mesh,
        in_specs=in_specs,
        out_specs=(P(both, None), P(both)),
        check_vma=False,
    )
```
